32 devices in a mesh: sec: 8 (over z, y), ops: 4 (over x, core).
Axes of the slice: x: 2, y: 2, z: 4, core: 2. Of those that a mesh axis runs over, the one named last changes fastest.
Arguments:
- wavefunction: bfloat16 [32, 32, 256, 256], P('sec'), may hold values from -6 to 6
- left_ops: bfloat16 [8, 32, 256, 256], P('ops', 'sec'), may hold values from -0.375 to 0.375
- right_ops: bfloat16 [8, 32, 256, 256], P('ops', 'sec'), may hold values from -0.125 to 0.125
- left_sizes: int32 [32], replicated, may hold values from 64 to 256, as said below
- right_sizes: int32 [32], replicated, may hold values from 64 to 256, as said below
- links: int32 [32, 32], replicated, may hold values 0 or 1
Outputs:
- sigma: bfloat16 [32, 32, 256, 256], P('ops', 'sec')
The draws below stay inside these ranges and needn't reach their ends.
Inputs may be any that keep to these rules, and one draw needn't show every extreme that they name: `left_sizes`: some sector has exactly 256 states. `right_sizes`: some sector has exactly 256 states.
All inputs are finite; a program needn't handle non-finite values.
Results may differ from the reference program's by a relative error of at most 0.005.
Values may be sent and summed in bfloat16 or wider, within the bound.
No kernel may reach another device: no remote copies, remote signals or barrier semaphores. Data moves between devices by JAX's collectives and lax.ppermute only.
A program may use at most 192 MiB of HBM per device.

```python
import jax
import jax.numpy as jnp
from jax import lax

B = 256
S = 32
K = 8


def sized_draw(key):
    first, second = jax.random.split(key)
    counts = jax.random.randint(first, (S,), B // 4, B + 1)
    spot = jax.random.randint(second, (), 0, S)
    return jnp.where(jnp.arange(S) == spot, B, counts).astype(jnp.int32)


def draw_left_sizes(key, part):
    key = jax.random.fold_in(key, 11)
    return sized_draw(key)


def draw_right_sizes(key, part):
    key = jax.random.fold_in(key, 23)
    return sized_draw(key)


def with_ends(drawn, own_key, least, high):
    spot = [jax.random.randint(jax.random.fold_in(own_key, axis), (), 0, length) for axis, length in enumerate(drawn.shape)]
    main_axis = drawn.shape.index(max(drawn.shape))
    neighbour = spot[:main_axis] + [(spot[main_axis] + 1) % drawn.shape[main_axis]] + spot[main_axis + 1:]
    return drawn.at[tuple(spot)].set(least).at[tuple(neighbour)].set(high)


def block_scale(key, extent, shards, least, top_value):
    loudness, own = 1.0, jax.random.fold_in(key, 6)
    for axis_at, blocks in shards:
        steps = jnp.exp(jax.random.uniform(jax.random.fold_in(own, axis_at), (blocks,), jnp.float32, least / len(shards), top_value / len(shards)))
        loudness = loudness * jnp.repeat(steps, extent[axis_at] // blocks).reshape([-1 if axis == axis_at else 1 for axis in range(len(extent))])
    return loudness


def noise(stream_key, shape, scale, most, cuts=(), kind=jnp.bfloat16):
    result = jax.random.normal(stream_key, shape, jnp.float32) * scale
    if len(cuts) > 0:
        result = block_scale(stream_key, shape, cuts, -0.22, 0.18) * result
    return jnp.clip(result, min=-most, max=most).astype(kind)


def setup_inputs(seed: int = 0) -> dict:
    streams_of = jax.random.split(jax.random.key(seed), 7)
    wavefunction = noise(streams_of[0], (S, S, B, B), 1.0, 6.0, ((0, 8),))
    left_ops = noise(streams_of[1], (K, S, B, B), B ** -0.5, 0.375, ((0, 4), (1, 8)))
    right_ops = noise(streams_of[2], (K, S, B, B), (B * K) ** -0.5, 0.125, ((0, 4), (1, 8)))
    left_sizes = draw_left_sizes(jax.random.fold_in(streams_of[6], 71), 0)
    right_sizes = draw_right_sizes(jax.random.fold_in(streams_of[6], 71), 0)
    links = with_ends((jax.random.randint(streams_of[5], (S, S), 0, 3) < 1).astype(jnp.int32), jax.random.fold_in(streams_of[5], 1), 0, 1)
    return dict(wavefunction=wavefunction, left_ops=left_ops, right_ops=right_ops, left_sizes=left_sizes, right_sizes=right_sizes, links=links)


def reference(wavefunction, left_ops, right_ops, left_sizes, right_sizes, links):
    states = jnp.arange(B, dtype=jnp.int32)
    left_mask = (states[None, :] < left_sizes[:, None]).astype(jnp.float32)
    right_mask = (states[None, :] < right_sizes[:, None]).astype(jnp.float32)
    keep = links.astype(jnp.float32)[:, :, None, None] * left_mask[:, None, :, None] * right_mask[None, :, None, :]
    psi = (wavefunction.astype(jnp.float32) * keep).astype(jnp.bfloat16)
    psi_wide = psi.astype(jnp.float32)

    def one_term(total, pair):
        left_block, right_block = pair
        upper = jnp.einsum('qab,qrbc->qrac', left_block.astype(jnp.float32), psi_wide).astype(jnp.bfloat16)
        term = jnp.einsum('qrac,rdc->qrad', upper.astype(jnp.float32), right_block.astype(jnp.float32))
        return total + term, None

    start = jnp.zeros((S, S, B, B), jnp.float32)
    total, unused = lax.scan(one_term, start, (left_ops, right_ops))
    return (total * keep).astype(jnp.bfloat16)
```

```python
import functools

import jax
import jax.numpy as jnp
from jax import lax
from jax.experimental import pallas as pl
from jax.experimental.pallas import tpu as pltpu
from jax.sharding import Mesh, PartitionSpec as P

SPLITS = 2


def generic(wavefunction, left_ops, right_ops, left_sizes, right_sizes, links):
    owned = wavefunction.shape[0]
    width = wavefunction.shape[2]
    first = lax.axis_index("sec") * owned
    states = jnp.arange(width, dtype=jnp.int32)
    left_mask = (states[None, :] < left_sizes[:, None]).astype(jnp.float32)
    right_mask = (states[None, :] < right_sizes[:, None]).astype(jnp.float32)
    links_wide = links.astype(jnp.float32)
    link_rows = lax.dynamic_slice_in_dim(links_wide, first, owned, 0)
    left_owned = lax.dynamic_slice_in_dim(left_mask, first, owned, 0)
    keep_left = (
        link_rows[:, :, None, None] * left_owned[:, None, :, None] * right_mask[None, :, None, :]
    )
    link_cols = lax.dynamic_slice_in_dim(links_wide, first, owned, 1)
    right_owned = lax.dynamic_slice_in_dim(right_mask, first, owned, 0)
    keep_right = (
        link_cols[:, :, None, None] * left_mask[:, None, :, None] * right_owned[None, :, None, :]
    )
    psi = jnp.where(keep_left > 0.0, wavefunction, jnp.zeros_like(wavefunction))
    psi_right = lax.all_to_all(psi, "sec", split_axis=1, concat_axis=0, tiled=True)
    full_left = lax.all_gather(left_ops, "sec", axis=1, tiled=True)
    upper = jnp.einsum(
        "kqab,qrbc->kqrac", full_left, psi_right, preferred_element_type=jnp.float32
    ).astype(jnp.bfloat16)
    total = jnp.einsum("kqrac,krdc->qrad", upper, right_ops, preferred_element_type=jnp.float32)
    summed = lax.psum_scatter(total, "ops", scatter_dimension=0, tiled=True)
    group_rows = summed.shape[0]
    keep_out = lax.dynamic_slice_in_dim(
        keep_right, lax.axis_index("ops") * group_rows, group_rows, 0
    )
    return (summed * keep_out).astype(jnp.bfloat16)


HEAD = 3


def block_kernel(planes, cols, terms, start, s_ref, l_refs, p_refs, r_ref, out_ref):
    f = pl.program_id(0)
    i = pl.program_id(1) + start
    z = s_ref[0]
    o = s_ref[2]
    sizes_at = HEAD + planes * 2 * cols
    nr = s_ref[sizes_at + planes + f * cols + i]
    width = out_ref.shape[-1]
    groups = planes
    per = terms // groups
    for d in range(planes):
        link = s_ref[HEAD + (d * 2 + f) * cols + i]
        nq = s_ref[sizes_at + d]
        slot = z ^ d

        @pl.when(link > 0)
        def _(d=d, nq=nq, slot=slot):
            rows = lax.broadcasted_iota(jnp.int32, (width, width), 0)
            lanes = lax.broadcasted_iota(jnp.int32, (width, width), 1)
            keep = (rows < nq) & (lanes < nr)
            psi = p_refs[d][0, 0]
            psi = jnp.where(keep, psi.astype(jnp.float32), 0.0).astype(jnp.bfloat16)
            total = jnp.zeros((width, width), jnp.float32)
            for e in range(groups):
                for kk in range(per):
                    left = l_refs[d][(o ^ e) * per + kk]
                    upper = jnp.dot(left, psi, preferred_element_type=jnp.float32)
                    total += lax.dot_general(
                        upper.astype(jnp.bfloat16),
                        r_ref[0, e * per + kk, 0],
                        (((1,), (1,)), ((), ())),
                        preferred_element_type=jnp.float32,
                    )
            out_ref[0, slot, 0] = jnp.where(keep, total, 0.0).astype(out_ref.dtype)

        @pl.when(link == 0)
        def _(slot=slot):
            out_ref[0, slot, 0] = jnp.zeros((width, width), out_ref.dtype)


def multiply(scalars, lefts, psis, rights, start, count):
    planes = len(lefts)
    terms, width = lefts[0].shape[0], lefts[0].shape[-1]
    cols = rights.shape[2]

    def body(s_ref, *refs):
        block_kernel(
            planes, cols, terms, start, s_ref, refs[:planes], refs[planes : 2 * planes],
            refs[2 * planes], refs[2 * planes + 1],
        )

    grid_spec = pltpu.PrefetchScalarGridSpec(
        num_scalar_prefetch=1,
        grid=(2, count),
        in_specs=[pl.BlockSpec((terms, width, width), lambda f, i, s: (0, 0, 0))] * planes
        + [pl.BlockSpec((1, 1, width, width), lambda f, i, s: (f ^ s[1], i + start, 0, 0))] * planes
        + [pl.BlockSpec((1, terms, 1, width, width), lambda f, i, s: (f, 0, i + start, 0, 0))],
        out_specs=pl.BlockSpec(
            (1, planes, 1, width, width), lambda f, i, s: (f ^ s[1], 0, i, 0, 0)
        ),
    )
    blocks = planes * 2 * count
    return pl.pallas_call(
        body,
        grid_spec=grid_spec,
        out_shape=jax.ShapeDtypeStruct((2, planes, count, width, width), jnp.bfloat16),
        compiler_params=pltpu.CompilerParams(vmem_limit_bytes=40 * 2**20),
        cost_estimate=pl.CostEstimate(
            flops=blocks * terms * 4 * width**3 // 3,
            bytes_accessed=(planes * terms + 2 * count * terms + 2 * blocks) * width * width * 2,
            transcendentals=0,
        ),
    )(scalars, *lefts, *psis, rights)


def planned(wavefunction, left_ops, right_ops, left_sizes, right_sizes, links):
    planes = lax.axis_size("o")
    z, y, o = lax.axis_index("z"), lax.axis_index("y"), lax.axis_index("o")
    owned, sectors = wavefunction.shape[:2]
    width = wavefunction.shape[-1]
    half = planes // 2
    plane_cols = sectors // planes
    cols = plane_cols // 2

    def along_z(value, pairs):
        return lax.ppermute(value, "z", pairs)

    def flip(value, axis, bit):
        size = lax.axis_size(axis)
        return lax.ppermute(value, axis, [(i, i ^ bit) for i in range(size)])

    row = lax.dynamic_index_in_dim(wavefunction, o, 0, keepdims=False)

    def columns_of(plane):
        return lax.dynamic_slice_in_dim(row, plane * plane_cols, plane_cols, 0)

    psis = [columns_of(z)]
    for d in range(1, planes):
        psis.append(
            lax.ppermute(columns_of(z ^ d), "z", [(i, i ^ d) for i in range(planes)])
        )
    psis = [p.reshape(2, cols, width, width) for p in psis]

    own = lax.all_to_all(left_ops, "o", split_axis=1, concat_axis=0, tiled=True)[:, 0]
    beside = flip(own, "z", 1)
    inner1 = along_z(own, [(1, 2), (2, 1)])
    inner2 = along_z(beside, [(1, 2), (2, 1)])
    outer1 = along_z(inner1, [(1, 0), (2, 3)])
    outer2 = along_z(inner2, [(1, 0), (2, 3)])
    inside = (z == 1) | (z == 2)
    lefts = [own, beside, jnp.where(inside, inner2, outer1), jnp.where(inside, inner1, outer2)]

    def swap_core(value):
        return flip(value, "o", 1)

    def swap_x(value):
        return flip(value, "o", 2)

    def swap_y(value):
        return flip(value, "y", 1)

    r_y = swap_y(right_ops)
    r_x = swap_x(right_ops)
    per = right_ops.shape[0]
    r_xy = jnp.concatenate([swap_y(r_x[: per // 2]), swap_x(r_y[per // 2 :])], axis=0)
    near = jnp.stack([right_ops, r_y])
    far = jnp.stack([r_x, r_xy])
    rights = jnp.concatenate([near, swap_core(near), far, swap_core(far)], axis=1)

    q_of = ((z ^ jnp.arange(planes)) * 2 + y) * owned + o
    r_of = (z * 2 + (y ^ jnp.arange(2)))[:, None] * cols + jnp.arange(cols)[None, :]
    r_of = r_of.reshape(-1)
    flags = (links[q_of][:, r_of] != 0).astype(jnp.int32)
    scalars = jnp.concatenate(
        [
            jnp.stack([z, y, o]).astype(jnp.int32),
            flags.reshape(-1),
            left_sizes[q_of],
            right_sizes[r_of],
        ]
    )

    parts = []
    count = cols // SPLITS
    for part in range(SPLITS):
        done = multiply(scalars, lefts, psis, rights, part * count, count)
        done = done.reshape(2 * planes, count, width, width)
        parts.append(
            lax.all_to_all(done, ("y", "o"), split_axis=0, concat_axis=0, tiled=True)
        )
    return jnp.concatenate(parts, axis=1)


def solution(mesh):
    sec, ops = mesh.shape["sec"], mesh.shape["ops"]

    def run(wavefunction, *rest):
        sectors = wavefunction.shape[0]
        if ops == 4 and sec == 2 * ops and sectors == sec * ops:
            where = Mesh(mesh.devices.reshape(sec // 2, 2, ops), ("z", "y", "o"))
            side, group, body = ("z", "y"), "o", planned
        else:
            where, side, group, body = mesh, "sec", "ops", generic
        placed = (
            P(side, None, None, None),
            P(group, side, None, None),
            P(group, side, None, None),
            P(),
            P(),
            P(),
        )
        return jax.shard_map(
            body, mesh=where, in_specs=placed, out_specs=P(group, side, None, None), check_vma=False
        )(wavefunction, *rest)

    return run
```

```python
import functools

import jax
import jax.numpy as jnp
from jax import lax
from jax.experimental import pallas as pl
from jax.experimental.pallas import tpu as pltpu
from jax.sharding import Mesh, PartitionSpec as P

def generic(wavefunction, left_ops, right_ops, left_sizes, right_sizes, links):
    owned = wavefunction.shape[0]
    width = wavefunction.shape[2]
    first = lax.axis_index("sec") * owned
    states = jnp.arange(width, dtype=jnp.int32)
    left_mask = (states[None, :] < left_sizes[:, None]).astype(jnp.float32)
    right_mask = (states[None, :] < right_sizes[:, None]).astype(jnp.float32)
    links_wide = links.astype(jnp.float32)
    link_rows = lax.dynamic_slice_in_dim(links_wide, first, owned, 0)
    left_owned = lax.dynamic_slice_in_dim(left_mask, first, owned, 0)
    keep_left = (
        link_rows[:, :, None, None] * left_owned[:, None, :, None] * right_mask[None, :, None, :]
    )
    link_cols = lax.dynamic_slice_in_dim(links_wide, first, owned, 1)
    right_owned = lax.dynamic_slice_in_dim(right_mask, first, owned, 0)
    keep_right = (
        link_cols[:, :, None, None] * left_mask[:, None, :, None] * right_owned[None, :, None, :]
    )
    psi = jnp.where(keep_left > 0.0, wavefunction, jnp.zeros_like(wavefunction))
    psi_right = lax.all_to_all(psi, "sec", split_axis=1, concat_axis=0, tiled=True)
    full_left = lax.all_gather(left_ops, "sec", axis=1, tiled=True)
    upper = jnp.einsum(
        "kqab,qrbc->kqrac", full_left, psi_right, preferred_element_type=jnp.float32
    ).astype(jnp.bfloat16)
    total = jnp.einsum("kqrac,krdc->qrad", upper, right_ops, preferred_element_type=jnp.float32)
    summed = lax.psum_scatter(total, "ops", scatter_dimension=0, tiled=True)
    group_rows = summed.shape[0]
    keep_out = lax.dynamic_slice_in_dim(
        keep_right, lax.axis_index("ops") * group_rows, group_rows, 0
    )
    return (summed * keep_out).astype(jnp.bfloat16)


HEAD = 4
GROUPS = ((0, 2), (1, 3))


def block_kernel(
    group, planes, cols, terms, pieces, slots_at, s_ref, l_refs, p_refs, r_refs, out_ref
):
    f = pl.program_id(0)
    i = pl.program_id(1)
    z = s_ref[0]
    sizes_at = HEAD + planes * 2 * cols
    nr = s_ref[sizes_at + planes + f * cols + i]
    width = out_ref.shape[-1]
    per = terms // planes
    for at, d in enumerate(group):
        link = s_ref[HEAD + (d * 2 + f) * cols + i]
        nq = s_ref[sizes_at + d]
        slot = (z ^ d) // 2

        @pl.when(link > 0)
        def _(at=at, d=d, nq=nq, slot=slot):
            rows = lax.broadcasted_iota(jnp.int32, (width, width), 0)
            lanes = lax.broadcasted_iota(jnp.int32, (width, width), 1)
            keep = (rows < nq) & (lanes < nr)
            if pieces[d] == [None]:
                psi = p_refs[at][0][0, 0]
            else:
                psi = p_refs[at][0][0]
                for (_, first, _), ref in zip(pieces[d][1:], p_refs[at][1:]):
                    held = s_ref[slots_at + (d * 2 + f) * cols + i] >= first
                    psi = jnp.where(held, ref[0], psi)
            psi = jnp.where(keep, psi.astype(jnp.float32), 0.0).astype(jnp.bfloat16)
            total = jnp.zeros((width, width), jnp.float32)
            for e in range(planes):
                for kk in range(per):
                    left = l_refs[at][e * per + kk]
                    upper = jnp.dot(left, psi, preferred_element_type=jnp.float32)
                    total += lax.dot_general(
                        upper.astype(jnp.bfloat16),
                        r_refs[e % 2][0, e // 2, kk, 0],
                        (((1,), (1,)), ((), ())),
                        preferred_element_type=jnp.float32,
                    )
            out_ref[0, slot, 0] = jnp.where(keep, total, 0.0).astype(out_ref.dtype)

        @pl.when(link == 0)
        def _(slot=slot):
            out_ref[0, slot, 0] = jnp.zeros((width, width), out_ref.dtype)


def multiply(group, room, scalars, lefts, psis, rights):
    terms, width = lefts[0].shape[0], lefts[0].shape[-1]
    cols = rights[0].shape[3]
    per = rights[0].shape[2]
    many = len(group)
    planes = terms // per

    slots_at = HEAD + planes * 2 * cols + planes + 2 * cols
    pieces = {d: [piece for piece in ranges(room) if piece[0] == d] or [None] for d in group}

    def body(s_ref, *refs):
        l_refs, p_refs, at = refs[:many], [], many
        for d in group:
            p_refs.append(refs[at : at + len(pieces[d])])
            at += len(pieces[d])
        block_kernel(
            group, planes, cols, terms, pieces, slots_at, s_ref, l_refs, p_refs,
            refs[at:-1], refs[-1],
        )

    def psi_spec(d, piece):
        if piece is None:
            return pl.BlockSpec(
                (1, 1, width, width),
                lambda f, i, s: (s[2] * 2 + s[3], (s[0] * 2 + (f ^ s[1])) * cols + i, 0, 0),
            )
        _, first, count = piece

        def index(f, i, s):
            slot = s[slots_at + (d * 2 + f) * cols + i]
            return (jnp.clip(slot - first, 0, count - 1), 0, 0)

        return pl.BlockSpec((1, width, width), index)

    grid_spec = pltpu.PrefetchScalarGridSpec(
        num_scalar_prefetch=1,
        grid=(2, cols),
        in_specs=[pl.BlockSpec((terms, width, width), lambda f, i, s: (0, 0, 0))] * many
        + [psi_spec(d, piece) for d in group for piece in pieces[d]]
        + [
            pl.BlockSpec((1, 2, per, 1, width, width), lambda f, i, s: (f, 0, 0, i, 0, 0))
        ]
        * 2,
        out_specs=pl.BlockSpec((1, 2, 1, width, width), lambda f, i, s: (f ^ s[1], 0, i, 0, 0)),
    )
    blocks = many * 2 * cols
    return pl.pallas_call(
        body,
        grid_spec=grid_spec,
        out_shape=jax.ShapeDtypeStruct((2, 2, cols, width, width), jnp.bfloat16),
        compiler_params=pltpu.CompilerParams(vmem_limit_bytes=48 * 2**20),
        cost_estimate=pl.CostEstimate(
            flops=blocks * terms * 4 * width**3 // 3,
            bytes_accessed=(many * terms + 2 * cols * terms + 2 * blocks) * width * width * 2,
            transcendentals=0,
        ),
    )(scalars, *lefts, *[piece for psi in psis for piece in psi], *rights)


def put_together(place, own_core, other_core):
    many, cols, width = own_core[0].shape[0], own_core[0].shape[1], own_core[0].shape[-1]

    def body(s_ref, *refs):
        out_ref = refs[-1]
        first = (s_ref[0] + s_ref[3]) % 2 == 0
        for at, mine in ((0, first), (1, jnp.logical_not(first))):

            @pl.when(mine)
            def _(at=at):
                out_ref[0, s_ref[3]] = refs[at][0]
                out_ref[0, 1 - s_ref[3]] = refs[2 + at][0]

    def block_of(at):
        def index(t, s):
            return (jnp.where((s[0] + s[3]) % 2 == at, t, 0), 0, 0, 0)

        return index

    return pl.pallas_call(
        body,
        grid_spec=pltpu.PrefetchScalarGridSpec(
            num_scalar_prefetch=1,
            grid=(many,),
            in_specs=[
                pl.BlockSpec((1, cols, width, width), block_of(at)) for at in (0, 1, 0, 1)
            ],
            out_specs=pl.BlockSpec((1, 2, cols, width, width), lambda t, s: (t, 0, 0, 0, 0)),
        ),
        out_shape=jax.ShapeDtypeStruct((many, 2, cols, width, width), own_core[0].dtype),
    )(place, *own_core, *other_core).reshape(2 * many, cols, width, width)


PIECES = {1: 1, 2: 2, 3: 2}


def ranges(room):
    out = []
    for d, many in PIECES.items():
        ends = [-(-room * at // many) for at in range(many + 1)]
        out += [(d, first, end - first) for first, end in zip(ends[:-1], ends[1:])]
    return out


def cut_out(cells, place, wavefunction, left_ops, planes, room):
    width = wavefunction.shape[-1]
    per = left_ops.shape[0]
    pieces = ranges(room)
    many = len(pieces)

    def body(c_ref, s_ref, *refs):
        half = len(refs) // 2
        for at in range(many):
            refs[half + at][0] = refs[at][0, 0]

        @pl.when(pl.program_id(0) == 0)
        def _():
            for at in range(many, half):
                refs[half + at][...] = refs[at][:, 0]

    def block_of(d, first, count):
        def index(t, c, s):
            slot = first + jnp.minimum(t, count - 1)
            return (s[2] * 2 + s[3], c[d * room + slot], 0, 0)

        return index

    def place_of(count):
        return lambda t, c, s: (jnp.minimum(t, count - 1), 0, 0)

    def sector_of(e):
        return lambda t, c, s: (0, (s[2] * 2 + s[3]) ^ e, 0, 0)

    outs = pl.pallas_call(
        body,
        grid_spec=pltpu.PrefetchScalarGridSpec(
            num_scalar_prefetch=2,
            grid=(max(count for _, _, count in pieces),),
            in_specs=[pl.BlockSpec((1, 1, width, width), block_of(*piece)) for piece in pieces]
            + [pl.BlockSpec((per, 1, width, width), sector_of(e)) for e in range(planes)],
            out_specs=[pl.BlockSpec((1, width, width), place_of(count)) for _, _, count in pieces]
            + [pl.BlockSpec((per, width, width), lambda t, c, s: (0, 0, 0))] * planes,
        ),
        out_shape=[
            jax.ShapeDtypeStruct((count, width, width), wavefunction.dtype)
            for _, _, count in pieces
        ]
        + [jax.ShapeDtypeStruct((per, width, width), left_ops.dtype)] * planes,
    )(cells, place, *([wavefunction] * many), *([left_ops] * planes))
    return outs[:many], outs[many:]


def running(mask):
    size = mask.shape[-1]
    upto = jnp.arange(size)[:, None] >= jnp.arange(size)[None, :]
    return jnp.sum(jnp.where(upto, mask[..., None, :], 0), axis=-1)


def planned(room, place, cell_table, scalars, wavefunction, left_ops, right_ops):
    planes = lax.axis_size("z")
    z, y, x, c = (lax.axis_index(name) for name in ("z", "y", "x", "c"))
    owned, sectors = wavefunction.shape[:2]
    width = wavefunction.shape[-1]
    cols = sectors // planes // 2
    after = lax.optimization_barrier

    def inner(value):
        return lax.ppermute(value, "z", [(1, 2), (2, 1)])

    def outer(value):
        return lax.ppermute(value, "z", [(1, 0), (2, 3)])

    def flip(value, axis, bit):
        size = lax.axis_size(axis)
        return lax.ppermute(value, axis, [(i, i ^ bit) for i in range(size)])

    def on_ops(value, bit):
        pairs = [(i, i ^ bit) for i in range(planes)]
        return lax.ppermute(value, ("x", "c"), pairs)

    cells = cell_table[:, :room].reshape(-1)
    cuts, sectors_cut = cut_out(cells, place, wavefunction, left_ops, planes, room)
    mine = [sectors_cut[0]] + [on_ops(sectors_cut[e], e) for e in range(1, planes)]
    psis = {0: [wavefunction]}
    for (d, _, _), cut in zip(ranges(room), cuts):
        psis.setdefault(d, []).append(flip(cut, "z", d))
    r_y = flip(right_ops, "y", 1)
    r_x = flip(right_ops, "x", 1)
    mine, r_x, r_y, psis[1], psis[2][0] = after((mine, r_x, r_y, psis[1], psis[2][0]))
    per = right_ops.shape[0]
    r_xy1 = flip(r_x[: per // 2], "y", 1)
    r_xy2 = flip(r_y[per // 2 :], "x", 1)
    own = jnp.concatenate(mine, axis=0)
    beside = flip(own, "z", 1)
    inner1 = inner(own)
    beside, inner1, r_xy1, r_xy2, psis[2][1] = after((beside, inner1, r_xy1, r_xy2, psis[2][1]))
    r_xy = jnp.concatenate([r_xy1, r_xy2], axis=0)
    near = jnp.stack([right_ops, r_x, r_y, r_xy]).reshape(2, 2, *right_ops.shape)
    other = flip(near, "c", 1)
    inner2 = inner(beside)
    outer1 = outer(inner1)
    inner2, outer1, other, psis[3][0] = after((inner2, outer1, other, psis[3][0]))
    rights = [near, other]
    outer2 = outer(inner2)

    inside = (z == 1) | (z == 2)
    lefts = [own, beside, jnp.where(inside, inner2, outer1), jnp.where(inside, inner1, outer2)]

    own_core, other_core = [], []
    for group in GROUPS:
        done = multiply(
            group, room, scalars, [lefts[d] for d in group], [psis[d] for d in group], rights
        )
        done = done.reshape(4, cols, width, width)
        own_core.append(
            lax.all_to_all(done, ("y", "x"), split_axis=0, concat_axis=0, tiled=True)
        )
        other_core.append(flip(own_core[-1], "c", 1))
    return put_together(place, own_core, other_core)


def tables(wavefunction, left_sizes, right_sizes, links):
    planes = lax.axis_size("z")
    z, y, x, c = (lax.axis_index(name) for name in ("z", "y", "x", "c"))
    owned, sectors = wavefunction.shape[:2]
    plane_cols = sectors // planes
    cols = plane_cols // 2
    o = x * 2 + c
    place = jnp.stack([z, y, x, c]).astype(jnp.int32)
    flips = jnp.arange(planes)
    marks = (links != 0).astype(jnp.int32)
    by_row = marks.reshape(planes, 2, owned, planes, plane_cols)
    away = (flips[:, None] != flips[None, :])[:, None, None, :]
    most = jnp.max(jnp.where(away, jnp.sum(by_row, axis=-1), 0))

    sent = marks[(z * 2 + y) * owned + o].reshape(planes, plane_cols)[z ^ flips]
    slot = running(sent) - 1
    hit = (slot[:, None, :] == jnp.arange(plane_cols)[None, :, None]) & (sent[:, None, :] > 0)
    sector = (z ^ flips)[:, None] * plane_cols + jnp.arange(plane_cols)[None, :]
    cell_table = jnp.sum(jnp.where(hit, sector[:, None, :], 0), axis=-1).astype(jnp.int32)

    q_of = ((z ^ flips) * 2 + y) * owned + o
    come = lax.dynamic_slice_in_dim(marks[q_of], z * plane_cols, plane_cols, 1)
    slots = jnp.maximum(running(come) - 1, 0)

    def sided(table):
        table = table.reshape(planes, 2, cols)
        return jnp.where(y > 0, table[:, ::-1], table).reshape(-1)

    r_of = (z * 2 + (y ^ jnp.arange(2)))[:, None] * cols + jnp.arange(cols)[None, :]
    scalars = jnp.concatenate(
        [place, sided(come), left_sizes[q_of], right_sizes[r_of.reshape(-1)], sided(slots)]
    ).astype(jnp.int32)
    return most, place, cell_table, scalars


ROOMS = (5, 6, 7)


def sparse(wavefunction, left_ops, right_ops, left_sizes, right_sizes, links):
    most, *rest = tables(wavefunction, left_sizes, right_sizes, links)
    whole = wavefunction.shape[1] // lax.axis_size("z")
    rooms = [room for room in ROOMS if room < whole] + [whole]
    forms = [functools.partial(planned, room) for room in rooms]
    which = jnp.sum((most > jnp.array(rooms[:-1], jnp.int32)).astype(jnp.int32))
    return lax.switch(which, forms, *rest, wavefunction, left_ops, right_ops)


def solution(mesh):
    sec, ops = mesh.shape["sec"], mesh.shape["ops"]

    def run(wavefunction, *rest):
        sectors = wavefunction.shape[0]
        if ops == 4 and sec == 2 * ops and sectors == sec * ops:
            where = Mesh(mesh.devices.reshape(sec // 2, 2, ops // 2, 2), ("z", "y", "x", "c"))
            side, group, body = ("z", "y"), ("x", "c"), sparse
        else:
            where, side, group, body = mesh, "sec", "ops", generic
        placed = (
            P(side, None, None, None),
            P(group, side, None, None),
            P(group, side, None, None),
            P(),
            P(),
            P(),
        )
        return jax.shard_map(
            body, mesh=where, in_specs=placed, out_specs=P(group, side, None, None), check_vma=False
        )(wavefunction, *rest)

    return run
```

```python
import functools

import jax
import jax.numpy as jnp
from jax import lax
from jax.experimental import pallas as pl
from jax.experimental.pallas import tpu as pltpu
from jax.sharding import Mesh, PartitionSpec as P

def generic(wavefunction, left_ops, right_ops, left_sizes, right_sizes, links):
    owned = wavefunction.shape[0]
    width = wavefunction.shape[2]
    first = lax.axis_index("sec") * owned
    states = jnp.arange(width, dtype=jnp.int32)
    left_mask = (states[None, :] < left_sizes[:, None]).astype(jnp.float32)
    right_mask = (states[None, :] < right_sizes[:, None]).astype(jnp.float32)
    links_wide = links.astype(jnp.float32)
    link_rows = lax.dynamic_slice_in_dim(links_wide, first, owned, 0)
    left_owned = lax.dynamic_slice_in_dim(left_mask, first, owned, 0)
    keep_left = (
        link_rows[:, :, None, None] * left_owned[:, None, :, None] * right_mask[None, :, None, :]
    )
    link_cols = lax.dynamic_slice_in_dim(links_wide, first, owned, 1)
    right_owned = lax.dynamic_slice_in_dim(right_mask, first, owned, 0)
    keep_right = (
        link_cols[:, :, None, None] * left_mask[:, None, :, None] * right_owned[None, :, None, :]
    )
    psi = jnp.where(keep_left > 0.0, wavefunction, jnp.zeros_like(wavefunction))
    psi_right = lax.all_to_all(psi, "sec", split_axis=1, concat_axis=0, tiled=True)
    full_left = lax.all_gather(left_ops, "sec", axis=1, tiled=True)
    upper = jnp.einsum(
        "kqab,qrbc->kqrac", full_left, psi_right, preferred_element_type=jnp.float32
    ).astype(jnp.bfloat16)
    total = jnp.einsum("kqrac,krdc->qrad", upper, right_ops, preferred_element_type=jnp.float32)
    summed = lax.psum_scatter(total, "ops", scatter_dimension=0, tiled=True)
    group_rows = summed.shape[0]
    keep_out = lax.dynamic_slice_in_dim(
        keep_right, lax.axis_index("ops") * group_rows, group_rows, 0
    )
    return (summed * keep_out).astype(jnp.bfloat16)


HEAD = 4
GROUPS = ((0, 2), (1, 3))


def block_kernel(
    d, planes, cols, terms, pieces, slots_at, s_ref, l_ref, p_refs, r_refs, out_ref
):
    f = pl.program_id(0)
    i = pl.program_id(1)
    sizes_at = HEAD + planes * 2 * cols
    nr = s_ref[sizes_at + planes + f * cols + i]
    width = out_ref.shape[-1]
    per = terms // planes
    link = s_ref[HEAD + (d * 2 + f) * cols + i]
    nq = s_ref[sizes_at + d]

    @pl.when(link > 0)
    def _():
        rows = lax.broadcasted_iota(jnp.int32, (width, width), 0)
        lanes = lax.broadcasted_iota(jnp.int32, (width, width), 1)
        keep = (rows < nq) & (lanes < nr)
        if d == 0:
            psi = p_refs[0][0, 0]
        else:
            psi = p_refs[0][0]
            for (_, first, _), ref in zip(pieces[1:], p_refs[1:]):
                held = s_ref[slots_at + (d * 2 + f) * cols + i] >= first
                psi = jnp.where(held, ref[0], psi)
        psi = jnp.where(keep, psi.astype(jnp.float32), 0.0).astype(jnp.bfloat16)
        total = jnp.zeros((width, width), jnp.float32)
        for e in range(planes):
            for kk in range(per):
                left = l_ref[e * per + kk]
                upper = jnp.dot(left, psi, preferred_element_type=jnp.float32)
                total += lax.dot_general(
                    upper.astype(jnp.bfloat16),
                    r_refs[e % 2][0, e // 2, kk, 0],
                    (((1,), (1,)), ((), ())),
                    preferred_element_type=jnp.float32,
                )
        out_ref[0, 0, 0] = jnp.where(keep, total, 0.0).astype(out_ref.dtype)

    @pl.when(link == 0)
    def _():
        out_ref[0, 0, 0] = jnp.zeros((width, width), out_ref.dtype)


def multiply(d, room, scalars, left, psis, rights, beside=None):
    terms, width = left.shape[0], left.shape[-1]
    cols = rights[0].shape[3]
    per = rights[0].shape[2]
    planes = terms // per
    slots_at = HEAD + planes * 2 * cols + planes + 2 * cols
    pieces = [piece for piece in ranges(room) if piece[0] == d] or [None]
    many = len(pieces)

    def body(s_ref, *refs):
        block_kernel(
            d, planes, cols, terms, pieces, slots_at, s_ref, refs[0], refs[1 : 1 + many],
            refs[1 + many : 3 + many], refs[-1],
        )

    def held(f, i, s):
        return s[slots_at + planes * 2 * cols + (d * 2 + f) * cols + i]

    def psi_spec(piece):
        if piece is None:
            return pl.BlockSpec(
                (1, 1, width, width),
                lambda f, i, s: (
                    s[2] * 2 + s[3],
                    (s[0] * 2 + (held(f, i, s) // cols ^ s[1])) * cols + held(f, i, s) % cols,
                    0,
                    0,
                ),
            )
        _, first, count = piece

        def index(f, i, s):
            slot = s[slots_at + (d * 2 + f) * cols + i]
            return (jnp.clip(slot - first, 0, count - 1), 0, 0)

        return pl.BlockSpec((1, width, width), index)

    in_specs = [pl.BlockSpec((terms, width, width), lambda f, i, s: (0, 0, 0))]
    in_specs += [psi_spec(piece) for piece in pieces]
    in_specs += [
        pl.BlockSpec(
            (1, 2, per, 1, width, width),
            lambda f, i, s: (held(f, i, s) // cols, 0, 0, held(f, i, s) % cols, 0, 0),
        )
    ] * 2
    inputs = [scalars, left, *psis, *rights]
    aliases = {}
    if beside is not None:
        in_specs.append(pl.BlockSpec(memory_space=pl.ANY))
        aliases = {len(inputs): 0}
        inputs.append(beside)
    blocks = 2 * cols
    return pl.pallas_call(
        body,
        grid_spec=pltpu.PrefetchScalarGridSpec(
            num_scalar_prefetch=1,
            grid=(2, cols),
            in_specs=in_specs,
            out_specs=pl.BlockSpec(
                (1, 1, 1, width, width), lambda f, i, s: (f ^ s[1], (s[0] ^ d) // 2, i, 0, 0)
            ),
        ),
        out_shape=jax.ShapeDtypeStruct((2, 2, cols, width, width), jnp.bfloat16),
        input_output_aliases=aliases,
        compiler_params=pltpu.CompilerParams(vmem_limit_bytes=48 * 2**20),
        cost_estimate=pl.CostEstimate(
            flops=blocks * terms * 16 * width**3,
            bytes_accessed=(terms + blocks * terms + 2 * blocks) * width * width * 2,
            transcendentals=0,
        ),
    )(*inputs)


def put_together(place, own_core, other_core):
    many, cols, width = own_core[0].shape[0], own_core[0].shape[1], own_core[0].shape[-1]

    def body(s_ref, *refs):
        out_ref = refs[-1]
        first = (s_ref[0] + s_ref[3]) % 2 == 0
        for at, mine in ((0, first), (1, jnp.logical_not(first))):

            @pl.when(mine)
            def _(at=at):
                out_ref[0, s_ref[3]] = refs[at][0]
                out_ref[0, 1 - s_ref[3]] = refs[2 + at][0]

    def block_of(at):
        def index(t, s):
            return (jnp.where((s[0] + s[3]) % 2 == at, t, 0), 0, 0, 0)

        return index

    return pl.pallas_call(
        body,
        grid_spec=pltpu.PrefetchScalarGridSpec(
            num_scalar_prefetch=1,
            grid=(many,),
            in_specs=[
                pl.BlockSpec((1, cols, width, width), block_of(at)) for at in (0, 1, 0, 1)
            ],
            out_specs=pl.BlockSpec((1, 2, cols, width, width), lambda t, s: (t, 0, 0, 0, 0)),
        ),
        out_shape=jax.ShapeDtypeStruct((many, 2, cols, width, width), own_core[0].dtype),
    )(place, *own_core, *other_core).reshape(2 * many, cols, width, width)


PIECES = {1: 1, 2: 2, 3: 2}


def ranges(room):
    out = []
    for d, many in PIECES.items():
        ends = [-(-room * at // many) for at in range(many + 1)]
        out += [(d, first, end - first) for first, end in zip(ends[:-1], ends[1:])]
    return out


def cut_out(cells, place, wavefunction, left_ops, planes, room):
    width = wavefunction.shape[-1]
    per = left_ops.shape[0]
    pieces = ranges(room)
    many = len(pieces)

    def body(c_ref, s_ref, *refs):
        half = many + planes
        for at in range(many):
            refs[half + at][0] = refs[at][0, 0]

        @pl.when(pl.program_id(0) == 0)
        def _():
            kept, to_core, to_chip = refs[half + many :]
            kept[...] = refs[many][:, 0]
            to_core[:per] = refs[many + 1][:, 0]
            to_core[per:] = refs[many + 3][:, 0]
            to_chip[...] = refs[many + 2][:, 0]

    def block_of(d, first, count):
        def index(t, c, s):
            slot = first + jnp.minimum(t, count - 1)
            return (s[2] * 2 + s[3], c[d * room + slot], 0, 0)

        return index

    def place_of(count):
        return lambda t, c, s: (jnp.minimum(t, count - 1), 0, 0)

    def sector_of(e):
        return lambda t, c, s: (0, (s[2] * 2 + s[3]) ^ e, 0, 0)

    outs = pl.pallas_call(
        body,
        grid_spec=pltpu.PrefetchScalarGridSpec(
            num_scalar_prefetch=2,
            grid=(max(count for _, _, count in pieces),),
            in_specs=[pl.BlockSpec((1, 1, width, width), block_of(*piece)) for piece in pieces]
            + [pl.BlockSpec((per, 1, width, width), sector_of(e)) for e in range(planes)],
            out_specs=[pl.BlockSpec((1, width, width), place_of(count)) for _, _, count in pieces]
            + [
                pl.BlockSpec((per * many, width, width), lambda t, c, s: (0, 0, 0))
                for many in (1, 2, 1)
            ],
        ),
        out_shape=[
            jax.ShapeDtypeStruct((count, width, width), wavefunction.dtype)
            for _, _, count in pieces
        ]
        + [
            jax.ShapeDtypeStruct((per * many, width, width), left_ops.dtype) for many in (1, 2, 1)
        ],
    )(cells, place, *([wavefunction] * many), *([left_ops] * planes))
    return outs[:many], outs[many:]


def running(mask):
    size = mask.shape[-1]
    upto = jnp.arange(size)[:, None] >= jnp.arange(size)[None, :]
    return jnp.sum(jnp.where(upto, mask[..., None, :], 0), axis=-1)


def planned(
    room, place, cell_table, left_sizes, right_sizes, links, wavefunction, left_ops, right_ops
):
    planes = lax.axis_size("z")
    z = lax.axis_index("z")
    sectors = wavefunction.shape[1]
    width = wavefunction.shape[-1]
    cols = sectors // planes // 2
    after = lax.optimization_barrier

    def inner(value):
        return lax.ppermute(value, "z", [(1, 2), (2, 1)])

    def outer(value):
        return lax.ppermute(value, "z", [(1, 0), (2, 3)])

    def flip(value, axis, bit):
        size = lax.axis_size(axis)
        return lax.ppermute(value, axis, [(i, i ^ bit) for i in range(size)])

    per = left_ops.shape[0]
    scalars = kernel_scalars(place, wavefunction.shape[0], left_sizes, right_sizes, links)
    cells = cell_table[:, :room].reshape(-1)
    cuts, sectors_cut = cut_out(cells, place, wavefunction, left_ops, planes, room)
    cuts, sectors_cut, right_ops = after((cuts, sectors_cut, right_ops))
    kept, to_core, to_chip = sectors_cut
    from_core = flip(to_core, "c", 1)
    from_chip = flip(jnp.concatenate([to_chip, from_core[per:]], axis=0), "x", 1)
    mine = [kept, from_core[:per], from_chip]
    psis = {0: [wavefunction]}
    late = cuts[-1]
    for (d, _, _), cut in zip(ranges(room)[:-1], cuts):
        psis.setdefault(d, []).append(flip(cut, "z", d))
    r_y = flip(right_ops, "y", 1)
    r_x1 = flip(right_ops[: per // 2], "x", 1)
    rest = right_ops[per // 2 :]
    mine, rest, r_y, r_x1, psis[1], psis[2][0] = after((mine, rest, r_y, r_x1, psis[1], psis[2][0]))
    r_x2 = flip(rest, "x", 1)
    r_xy = flip(r_y, "x", 1)
    own = jnp.concatenate(mine, axis=0)
    beside = flip(own, "z", 1)
    inner1 = inner(own)
    beside, inner1, r_x2, r_xy, psis[2][1] = after((beside, inner1, r_x2, r_xy, psis[2][1]))
    r_x = jnp.concatenate([r_x1, r_x2], axis=0)
    near = jnp.stack([right_ops, r_x, r_y, r_xy]).reshape(2, 2, *right_ops.shape)
    other = flip(near, "c", 1)
    inner2 = inner(beside)
    outer1 = outer(inner1)
    rights = [near, other]
    lefts = [own, beside, None, None]
    firsts = [
        multiply(first, room, scalars, lefts[first], psis[first], rights) for first, _ in GROUPS
    ]
    inner2, outer1, firsts, late, psis[3][0] = after((inner2, outer1, firsts, late, psis[3][0]))
    outer2 = outer(inner2)
    psis[3].append(flip(late, "z", 3))

    inside = (z == 1) | (z == 2)
    lefts[2] = jnp.where(inside, inner2, outer1)
    lefts[3] = jnp.where(inside, inner1, outer2)

    own_core, other_core = [], []
    for (_, second), done in zip(GROUPS, firsts):
        done = multiply(second, room, scalars, lefts[second], psis[second], rights, done)
        done = done.reshape(4, cols, width, width)
        own_core.append(
            lax.all_to_all(done, ("y", "x"), split_axis=0, concat_axis=0, tiled=True)
        )
        other_core.append(flip(own_core[-1], "c", 1))
    return put_together(place, own_core, other_core)


def tables(wavefunction, links):
    planes = lax.axis_size("z")
    z, y, x, c = (lax.axis_index(name) for name in ("z", "y", "x", "c"))
    owned, sectors = wavefunction.shape[:2]
    plane_cols = sectors // planes
    o = x * 2 + c
    place = jnp.stack([z, y, x, c]).astype(jnp.int32)
    flips = jnp.arange(planes)
    marks = (links != 0).astype(jnp.int32)
    by_row = marks.reshape(planes, 2, owned, planes, plane_cols)
    away = (flips[:, None] != flips[None, :])[:, None, None, :]
    most = jnp.max(jnp.where(away, jnp.sum(by_row, axis=-1), 0))

    sent = marks[(z * 2 + y) * owned + o].reshape(planes, plane_cols)[z ^ flips]
    slot = running(sent) - 1
    hit = (slot[:, None, :] == jnp.arange(plane_cols)[None, :, None]) & (sent[:, None, :] > 0)
    sector = (z ^ flips)[:, None] * plane_cols + jnp.arange(plane_cols)[None, :]
    cell_table = jnp.sum(jnp.where(hit, sector[:, None, :], 0), axis=-1).astype(jnp.int32)

    return most, place, cell_table


def kernel_scalars(place, owned, left_sizes, right_sizes, links):
    planes = lax.axis_size("z")
    z, y, x, c = (lax.axis_index(name) for name in ("z", "y", "x", "c"))
    plane_cols = links.shape[1] // planes
    cols = plane_cols // 2
    marks = (links != 0).astype(jnp.int32)

    q_of = ((z ^ jnp.arange(planes)) * 2 + y) * owned + x * 2 + c
    come = lax.dynamic_slice_in_dim(marks[q_of], z * plane_cols, plane_cols, 1)
    slots = jnp.maximum(running(come) - 1, 0)

    def sided(table):
        table = table.reshape(planes, 2, cols)
        return jnp.where(y > 0, table[:, ::-1], table).reshape(planes, plane_cols)

    flags = sided(come)
    steps = jnp.arange(plane_cols)
    upto = (steps[:, None] >= steps[None, :]) & (flags[:, None, :] > 0)
    last = jnp.max(jnp.where(upto, steps, -1), axis=-1)
    first = jnp.min(jnp.where(flags > 0, steps, plane_cols - 1), axis=-1)
    held = jnp.where(last >= 0, last, first[:, None])
    r_of = (z * 2 + (y ^ jnp.arange(2)))[:, None] * cols + jnp.arange(cols)[None, :]
    parts = [place, flags, left_sizes[q_of], right_sizes[r_of.reshape(-1)], sided(slots), held]
    return jnp.concatenate([part.reshape(-1) for part in parts]).astype(jnp.int32)


ROOMS = (5, 6, 7)


def sparse(wavefunction, left_ops, right_ops, left_sizes, right_sizes, links):
    most, *rest = tables(wavefunction, links)
    rest += [left_sizes, right_sizes, links]
    whole = wavefunction.shape[1] // lax.axis_size("z")
    rooms = [room for room in ROOMS if room < whole] + [whole]
    forms = [functools.partial(planned, room) for room in rooms]
    which = jnp.sum((most > jnp.array(rooms[:-1], jnp.int32)).astype(jnp.int32))
    return lax.switch(which, forms, *rest, wavefunction, left_ops, right_ops)


def solution(mesh):
    sec, ops = mesh.shape["sec"], mesh.shape["ops"]

    def run(wavefunction, *rest):
        sectors = wavefunction.shape[0]
        if ops == 4 and sec == 2 * ops and sectors == sec * ops:
            where = Mesh(mesh.devices.reshape(sec // 2, 2, ops // 2, 2), ("z", "y", "x", "c"))
            side, group, body = ("z", "y"), ("x", "c"), sparse
        else:
            where, side, group, body = mesh, "sec", "ops", generic
        placed = (
            P(side, None, None, None),
            P(group, side, None, None),
            P(group, side, None, None),
            P(),
            P(),
            P(),
        )
        return jax.shard_map(
            body, mesh=where, in_specs=placed, out_specs=P(group, side, None, None), check_vma=False
        )(wavefunction, *rest)

    return run
```

```python
import functools

import jax
import jax.numpy as jnp
from jax import lax
from jax.experimental import pallas as pl
from jax.experimental.pallas import tpu as pltpu
from jax.sharding import Mesh, PartitionSpec as P

def generic(wavefunction, left_ops, right_ops, left_sizes, right_sizes, links):
    owned = wavefunction.shape[0]
    width = wavefunction.shape[2]
    first = lax.axis_index("sec") * owned
    states = jnp.arange(width, dtype=jnp.int32)
    left_mask = (states[None, :] < left_sizes[:, None]).astype(jnp.float32)
    right_mask = (states[None, :] < right_sizes[:, None]).astype(jnp.float32)
    links_wide = links.astype(jnp.float32)
    link_rows = lax.dynamic_slice_in_dim(links_wide, first, owned, 0)
    left_owned = lax.dynamic_slice_in_dim(left_mask, first, owned, 0)
    keep_left = (
        link_rows[:, :, None, None] * left_owned[:, None, :, None] * right_mask[None, :, None, :]
    )
    link_cols = lax.dynamic_slice_in_dim(links_wide, first, owned, 1)
    right_owned = lax.dynamic_slice_in_dim(right_mask, first, owned, 0)
    keep_right = (
        link_cols[:, :, None, None] * left_mask[:, None, :, None] * right_owned[None, :, None, :]
    )
    psi = jnp.where(keep_left > 0.0, wavefunction, jnp.zeros_like(wavefunction))
    psi_right = lax.all_to_all(psi, "sec", split_axis=1, concat_axis=0, tiled=True)
    full_left = lax.all_gather(left_ops, "sec", axis=1, tiled=True)
    upper = jnp.einsum(
        "kqab,qrbc->kqrac", full_left, psi_right, preferred_element_type=jnp.float32
    ).astype(jnp.bfloat16)
    total = jnp.einsum("kqrac,krdc->qrad", upper, right_ops, preferred_element_type=jnp.float32)
    summed = lax.psum_scatter(total, "ops", scatter_dimension=0, tiled=True)
    group_rows = summed.shape[0]
    keep_out = lax.dynamic_slice_in_dim(
        keep_right, lax.axis_index("ops") * group_rows, group_rows, 0
    )
    return (summed * keep_out).astype(jnp.bfloat16)


HEAD = 4
GROUPS = ((0, 2), (1, 3))


def block_kernel(
    d, planes, cols, terms, pieces, slots_at, s_ref, l_ref, p_refs, r_refs, out_ref
):
    f = pl.program_id(0)
    i = pl.program_id(1)
    sizes_at = HEAD + planes * 2 * cols
    nr = s_ref[sizes_at + planes + f * cols + i]
    width = out_ref.shape[-1]
    per = terms // planes
    link = s_ref[HEAD + (d * 2 + f) * cols + i]
    nq = s_ref[sizes_at + d]

    @pl.when(link > 0)
    def _():
        rows = lax.broadcasted_iota(jnp.int32, (width, width), 0)
        lanes = lax.broadcasted_iota(jnp.int32, (width, width), 1)
        keep = (rows < nq) & (lanes < nr)
        if d == 0:
            psi = p_refs[0][0, 0]
        else:
            psi = p_refs[0][0]
            for (_, first, _), ref in zip(pieces[1:], p_refs[1:]):
                held = s_ref[slots_at + (d * 2 + f) * cols + i] >= first
                psi = jnp.where(held, ref[0], psi)
        psi = jnp.where(keep, psi.astype(jnp.float32), 0.0).astype(jnp.bfloat16)
        total = jnp.zeros((width, width), jnp.float32)
        for e in range(planes):
            for kk in range(per):
                left = l_ref[e * per + kk]
                upper = jnp.dot(left, psi, preferred_element_type=jnp.float32)
                total += lax.dot_general(
                    upper.astype(jnp.bfloat16),
                    r_refs[e % 2][0, e // 2, kk, 0],
                    (((1,), (1,)), ((), ())),
                    preferred_element_type=jnp.float32,
                )
        out_ref[0, 0, 0] = jnp.where(keep, total, 0.0).astype(out_ref.dtype)

    @pl.when(link == 0)
    def _():
        out_ref[0, 0, 0] = jnp.zeros((width, width), out_ref.dtype)


def multiply(d, room, scalars, left, psis, rights, beside=None):
    terms, width = left.shape[0], left.shape[-1]
    cols = rights[0].shape[3]
    per = rights[0].shape[2]
    planes = terms // per
    slots_at = HEAD + planes * 2 * cols + planes + 2 * cols
    pieces = [piece for piece in ranges(room) if piece[0] == d] or [None]
    many = len(pieces)

    def body(s_ref, *refs):
        block_kernel(
            d, planes, cols, terms, pieces, slots_at, s_ref, refs[0], refs[1 : 1 + many],
            refs[1 + many : 3 + many], refs[-1],
        )

    def held(f, i, s):
        return s[slots_at + planes * 2 * cols + (d * 2 + f) * cols + i]

    def psi_spec(piece):
        if piece is None:
            return pl.BlockSpec(
                (1, 1, width, width),
                lambda f, i, s: (
                    s[2] * 2 + s[3],
                    (s[0] * 2 + (held(f, i, s) // cols ^ s[1])) * cols + held(f, i, s) % cols,
                    0,
                    0,
                ),
            )
        _, first, count = piece

        def index(f, i, s):
            slot = s[slots_at + (d * 2 + f) * cols + i]
            return (jnp.clip(slot - first, 0, count - 1), 0, 0)

        return pl.BlockSpec((1, width, width), index)

    in_specs = [pl.BlockSpec((terms, width, width), lambda f, i, s: (0, 0, 0))]
    in_specs += [psi_spec(piece) for piece in pieces]
    in_specs += [
        pl.BlockSpec(
            (1, 2, per, 1, width, width),
            lambda f, i, s: (held(f, i, s) // cols, 0, 0, held(f, i, s) % cols, 0, 0),
        )
    ] * 2
    inputs = [scalars, left, *psis, *rights]
    aliases = {}
    if beside is not None:
        in_specs.append(pl.BlockSpec(memory_space=pl.ANY))
        aliases = {len(inputs): 0}
        inputs.append(beside)
    blocks = 2 * cols
    return pl.pallas_call(
        body,
        grid_spec=pltpu.PrefetchScalarGridSpec(
            num_scalar_prefetch=1,
            grid=(2, cols),
            in_specs=in_specs,
            out_specs=pl.BlockSpec(
                (1, 1, 1, width, width), lambda f, i, s: (f ^ s[1], (s[0] ^ d) // 2, i, 0, 0)
            ),
        ),
        out_shape=jax.ShapeDtypeStruct((2, 2, cols, width, width), jnp.bfloat16),
        input_output_aliases=aliases,
        compiler_params=pltpu.CompilerParams(vmem_limit_bytes=48 * 2**20),
        cost_estimate=pl.CostEstimate(
            flops=blocks * terms * 16 * width**3,
            bytes_accessed=(terms + blocks * terms + 2 * blocks) * width * width * 2,
            transcendentals=0,
        ),
    )(*inputs)


def put_together(place, own_core, other_core):
    many, cols, width = own_core[0].shape[0], own_core[0].shape[1], own_core[0].shape[-1]

    def body(s_ref, *refs):
        out_ref = refs[-1]
        first = (s_ref[0] + s_ref[3]) % 2 == 0
        for at, mine in ((0, first), (1, jnp.logical_not(first))):

            @pl.when(mine)
            def _(at=at):
                out_ref[0, s_ref[3]] = refs[at][0]
                out_ref[0, 1 - s_ref[3]] = refs[2 + at][0]

    def block_of(at):
        def index(t, s):
            return (jnp.where((s[0] + s[3]) % 2 == at, t, 0), 0, 0, 0)

        return index

    return pl.pallas_call(
        body,
        grid_spec=pltpu.PrefetchScalarGridSpec(
            num_scalar_prefetch=1,
            grid=(many,),
            in_specs=[
                pl.BlockSpec((1, cols, width, width), block_of(at)) for at in (0, 1, 0, 1)
            ],
            out_specs=pl.BlockSpec((1, 2, cols, width, width), lambda t, s: (t, 0, 0, 0, 0)),
        ),
        out_shape=jax.ShapeDtypeStruct((many, 2, cols, width, width), own_core[0].dtype),
    )(place, *own_core, *other_core).reshape(2 * many, cols, width, width)


PIECES = {1: 1, 2: 2, 3: 2}


def ranges(room):
    out = []
    for d, many in PIECES.items():
        ends = [-(-room * at // many) for at in range(many + 1)]
        if many > 1:
            ends[1] += 1
        out += [(d, first, end - first) for first, end in zip(ends[:-1], ends[1:])]
    return out


def cut_out(cells, place, wavefunction, left_ops, planes, room):
    width = wavefunction.shape[-1]
    per = left_ops.shape[0]
    pieces = ranges(room)
    many = len(pieces)

    def body(c_ref, s_ref, *refs):
        half = many + planes
        for at in range(many):
            refs[half + at][0] = refs[at][0, 0]

        @pl.when(pl.program_id(0) == 0)
        def _():
            kept, to_core, to_chip = refs[half + many :]
            kept[...] = refs[many][:, 0]
            to_core[:per] = refs[many + 1][:, 0]
            to_core[per:] = refs[many + 3][:, 0]
            to_chip[...] = refs[many + 2][:, 0]

    def block_of(d, first, count):
        def index(t, c, s):
            slot = first + jnp.minimum(t, count - 1)
            return (s[2] * 2 + s[3], c[d * room + slot], 0, 0)

        return index

    def place_of(count):
        return lambda t, c, s: (jnp.minimum(t, count - 1), 0, 0)

    def sector_of(e):
        return lambda t, c, s: (0, (s[2] * 2 + s[3]) ^ e, 0, 0)

    outs = pl.pallas_call(
        body,
        grid_spec=pltpu.PrefetchScalarGridSpec(
            num_scalar_prefetch=2,
            grid=(max(count for _, _, count in pieces),),
            in_specs=[pl.BlockSpec((1, 1, width, width), block_of(*piece)) for piece in pieces]
            + [pl.BlockSpec((per, 1, width, width), sector_of(e)) for e in range(planes)],
            out_specs=[pl.BlockSpec((1, width, width), place_of(count)) for _, _, count in pieces]
            + [
                pl.BlockSpec((per * many, width, width), lambda t, c, s: (0, 0, 0))
                for many in (1, 2, 1)
            ],
        ),
        out_shape=[
            jax.ShapeDtypeStruct((count, width, width), wavefunction.dtype)
            for _, _, count in pieces
        ]
        + [
            jax.ShapeDtypeStruct((per * many, width, width), left_ops.dtype) for many in (1, 2, 1)
        ],
    )(cells, place, *([wavefunction] * many), *([left_ops] * planes))
    return outs[:many], outs[many:]


def running(mask):
    size = mask.shape[-1]
    upto = jnp.arange(size)[:, None] >= jnp.arange(size)[None, :]
    return jnp.sum(jnp.where(upto, mask[..., None, :], 0), axis=-1)


def planned(
    room, place, cell_table, left_sizes, right_sizes, links, wavefunction, left_ops, right_ops
):
    planes = lax.axis_size("z")
    z = lax.axis_index("z")
    sectors = wavefunction.shape[1]
    width = wavefunction.shape[-1]
    cols = sectors // planes // 2
    after = lax.optimization_barrier

    def inner(value):
        return lax.ppermute(value, "z", [(1, 2), (2, 1)])

    def outer(value):
        return lax.ppermute(value, "z", [(1, 0), (2, 3)])

    def flip(value, axis, bit):
        size = lax.axis_size(axis)
        return lax.ppermute(value, axis, [(i, i ^ bit) for i in range(size)])

    per = left_ops.shape[0]
    scalars = kernel_scalars(place, wavefunction.shape[0], left_sizes, right_sizes, links)
    cells = cell_table[:, :room].reshape(-1)
    cuts, sectors_cut = cut_out(cells, place, wavefunction, left_ops, planes, room)
    cuts, sectors_cut, right_ops = after((cuts, sectors_cut, right_ops))
    kept, to_core, to_chip = sectors_cut
    from_core = flip(to_core, "c", 1)
    from_chip = flip(jnp.concatenate([to_chip, from_core[per:]], axis=0), "x", 1)
    mine = [kept, from_core[:per], from_chip]
    psis = {0: [wavefunction]}
    late = cuts[-1]
    for (d, _, _), cut in zip(ranges(room)[:-1], cuts):
        psis.setdefault(d, []).append(flip(cut, "z", d))
    r_y = flip(right_ops, "y", 1)
    r_x1 = flip(right_ops[: per // 2], "x", 1)
    rest = right_ops[per // 2 :]
    mine, rest, r_y, r_x1, psis[1], psis[2][0] = after((mine, rest, r_y, r_x1, psis[1], psis[2][0]))
    r_x2 = flip(rest, "x", 1)
    r_xy = flip(r_y, "x", 1)
    own = jnp.concatenate(mine, axis=0)
    beside = flip(own, "z", 1)
    inner1 = inner(own)
    beside, inner1, r_x2, r_xy, psis[2][1] = after((beside, inner1, r_x2, r_xy, psis[2][1]))
    r_x = jnp.concatenate([r_x1, r_x2], axis=0)
    near = jnp.stack([right_ops, r_x, r_y, r_xy]).reshape(2, 2, *right_ops.shape)
    other = flip(near, "c", 1)
    inner2 = inner(beside)
    outer1 = outer(inner1)
    rights = [near, other]
    lefts = [own, beside, None, None]
    firsts = [
        multiply(first, room, scalars, lefts[first], psis[first], rights) for first, _ in GROUPS
    ]
    inner2, outer1, firsts, late, psis[3][0] = after((inner2, outer1, firsts, late, psis[3][0]))
    outer2 = outer(inner2)
    psis[3].append(flip(late, "z", 3))

    inside = (z == 1) | (z == 2)
    lefts[2] = jnp.where(inside, inner2, outer1)
    lefts[3] = jnp.where(inside, inner1, outer2)

    own_core, other_core = [], []
    for (_, second), done in zip(GROUPS, firsts):
        done = multiply(second, room, scalars, lefts[second], psis[second], rights, done)
        done = done.reshape(4, cols, width, width)
        own_core.append(
            lax.all_to_all(done, ("y", "x"), split_axis=0, concat_axis=0, tiled=True)
        )
        other_core.append(flip(own_core[-1], "c", 1))
    return put_together(place, own_core, other_core)


def tables(wavefunction, links):
    planes = lax.axis_size("z")
    z, y, x, c = (lax.axis_index(name) for name in ("z", "y", "x", "c"))
    owned, sectors = wavefunction.shape[:2]
    plane_cols = sectors // planes
    o = x * 2 + c
    place = jnp.stack([z, y, x, c]).astype(jnp.int32)
    flips = jnp.arange(planes)
    marks = (links != 0).astype(jnp.int32)
    by_row = marks.reshape(planes, 2, owned, planes, plane_cols)
    away = (flips[:, None] != flips[None, :])[:, None, None, :]
    most = jnp.max(jnp.where(away, jnp.sum(by_row, axis=-1), 0))

    sent = marks[(z * 2 + y) * owned + o].reshape(planes, plane_cols)[z ^ flips]
    slot = running(sent) - 1
    hit = (slot[:, None, :] == jnp.arange(plane_cols)[None, :, None]) & (sent[:, None, :] > 0)
    sector = (z ^ flips)[:, None] * plane_cols + jnp.arange(plane_cols)[None, :]
    cell_table = jnp.sum(jnp.where(hit, sector[:, None, :], 0), axis=-1).astype(jnp.int32)

    return most, place, cell_table


def kernel_scalars(place, owned, left_sizes, right_sizes, links):
    planes = lax.axis_size("z")
    z, y, x, c = (lax.axis_index(name) for name in ("z", "y", "x", "c"))
    plane_cols = links.shape[1] // planes
    cols = plane_cols // 2
    marks = (links != 0).astype(jnp.int32)

    q_of = ((z ^ jnp.arange(planes)) * 2 + y) * owned + x * 2 + c
    come = lax.dynamic_slice_in_dim(marks[q_of], z * plane_cols, plane_cols, 1)
    slots = jnp.maximum(running(come) - 1, 0)

    def sided(table):
        table = table.reshape(planes, 2, cols)
        return jnp.where(y > 0, table[:, ::-1], table).reshape(planes, plane_cols)

    flags = sided(come)
    steps = jnp.arange(plane_cols)
    upto = (steps[:, None] >= steps[None, :]) & (flags[:, None, :] > 0)
    last = jnp.max(jnp.where(upto, steps, -1), axis=-1)
    first = jnp.min(jnp.where(flags > 0, steps, plane_cols - 1), axis=-1)
    held = jnp.where(last >= 0, last, first[:, None])
    r_of = (z * 2 + (y ^ jnp.arange(2)))[:, None] * cols + jnp.arange(cols)[None, :]
    parts = [place, flags, left_sizes[q_of], right_sizes[r_of.reshape(-1)], sided(slots), held]
    return jnp.concatenate([part.reshape(-1) for part in parts]).astype(jnp.int32)


ROOMS = (5, 6, 7)


def sparse(wavefunction, left_ops, right_ops, left_sizes, right_sizes, links):
    most, *rest = tables(wavefunction, links)
    rest += [left_sizes, right_sizes, links]
    whole = wavefunction.shape[1] // lax.axis_size("z")
    rooms = [room for room in ROOMS if room < whole] + [whole]
    forms = [functools.partial(planned, room) for room in rooms]
    which = jnp.sum((most > jnp.array(rooms[:-1], jnp.int32)).astype(jnp.int32))
    return lax.switch(which, forms, *rest, wavefunction, left_ops, right_ops)


def solution(mesh):
    sec, ops = mesh.shape["sec"], mesh.shape["ops"]

    def run(wavefunction, *rest):
        sectors = wavefunction.shape[0]
        if ops == 4 and sec == 2 * ops and sectors == sec * ops:
            where = Mesh(mesh.devices.reshape(sec // 2, 2, ops // 2, 2), ("z", "y", "x", "c"))
            side, group, body = ("z", "y"), ("x", "c"), sparse
        else:
            where, side, group, body = mesh, "sec", "ops", generic
        placed = (
            P(side, None, None, None),
            P(group, side, None, None),
            P(group, side, None, None),
            P(),
            P(),
            P(),
        )
        return jax.shard_map(
            body, mesh=where, in_specs=placed, out_specs=P(group, side, None, None), check_vma=False
        )(wavefunction, *rest)

    return run
```

```python
import functools

import jax
import jax.numpy as jnp
from jax import lax
from jax.experimental import pallas as pl
from jax.experimental.pallas import tpu as pltpu
from jax.sharding import Mesh, PartitionSpec as P

def generic(wavefunction, left_ops, right_ops, left_sizes, right_sizes, links):
    owned = wavefunction.shape[0]
    width = wavefunction.shape[2]
    first = lax.axis_index("sec") * owned
    states = jnp.arange(width, dtype=jnp.int32)
    left_mask = (states[None, :] < left_sizes[:, None]).astype(jnp.float32)
    right_mask = (states[None, :] < right_sizes[:, None]).astype(jnp.float32)
    links_wide = links.astype(jnp.float32)
    link_rows = lax.dynamic_slice_in_dim(links_wide, first, owned, 0)
    left_owned = lax.dynamic_slice_in_dim(left_mask, first, owned, 0)
    keep_left = (
        link_rows[:, :, None, None] * left_owned[:, None, :, None] * right_mask[None, :, None, :]
    )
    link_cols = lax.dynamic_slice_in_dim(links_wide, first, owned, 1)
    right_owned = lax.dynamic_slice_in_dim(right_mask, first, owned, 0)
    keep_right = (
        link_cols[:, :, None, None] * left_mask[:, None, :, None] * right_owned[None, :, None, :]
    )
    psi = jnp.where(keep_left > 0.0, wavefunction, jnp.zeros_like(wavefunction))
    psi_right = lax.all_to_all(psi, "sec", split_axis=1, concat_axis=0, tiled=True)
    full_left = lax.all_gather(left_ops, "sec", axis=1, tiled=True)
    upper = jnp.einsum(
        "kqab,qrbc->kqrac", full_left, psi_right, preferred_element_type=jnp.float32
    ).astype(jnp.bfloat16)
    total = jnp.einsum("kqrac,krdc->qrad", upper, right_ops, preferred_element_type=jnp.float32)
    summed = lax.psum_scatter(total, "ops", scatter_dimension=0, tiled=True)
    group_rows = summed.shape[0]
    keep_out = lax.dynamic_slice_in_dim(
        keep_right, lax.axis_index("ops") * group_rows, group_rows, 0
    )
    return (summed * keep_out).astype(jnp.bfloat16)


HEAD = 4
GROUPS = ((0, 2), (1, 3))


def block_kernel(
    d, planes, cols, terms, pieces, slots_at, s_ref, l_ref, p_refs, r_refs, out_ref
):
    f = pl.program_id(0)
    i = pl.program_id(1)
    sizes_at = HEAD + planes * 2 * cols
    nr = s_ref[sizes_at + planes + f * cols + i]
    width = out_ref.shape[-1]
    per = terms // planes
    link = s_ref[HEAD + (d * 2 + f) * cols + i]
    nq = s_ref[sizes_at + d]

    @pl.when(link > 0)
    def _():
        rows = lax.broadcasted_iota(jnp.int32, (width, width), 0)
        lanes = lax.broadcasted_iota(jnp.int32, (width, width), 1)
        keep = (rows < nq) & (lanes < nr)
        if d == 0:
            psi = p_refs[0][0, 0]
        else:
            psi = p_refs[0][0]
            for (_, first, _), ref in zip(pieces[1:], p_refs[1:]):
                held = s_ref[slots_at + (d * 2 + f) * cols + i] >= first
                psi = jnp.where(held, ref[0], psi)
        psi = jnp.where(keep, psi.astype(jnp.float32), 0.0).astype(jnp.bfloat16)
        total = jnp.zeros((width, width), jnp.float32)
        for e in range(planes):
            for kk in range(per):
                left = l_ref[e * per + kk]
                upper = jnp.dot(left, psi, preferred_element_type=jnp.float32)
                total += lax.dot_general(
                    upper.astype(jnp.bfloat16),
                    r_refs[e % 2][0, e // 2, kk, 0],
                    (((1,), (1,)), ((), ())),
                    preferred_element_type=jnp.float32,
                )
        out_ref[0, 0, 0] = jnp.where(keep, total, 0.0).astype(out_ref.dtype)

    @pl.when(link == 0)
    def _():
        out_ref[0, 0, 0] = jnp.zeros((width, width), out_ref.dtype)


def multiply(d, room, scalars, left, psis, rights, beside=None):
    terms, width = left.shape[0], left.shape[-1]
    cols = rights[0].shape[3]
    per = rights[0].shape[2]
    planes = terms // per
    slots_at = HEAD + planes * 2 * cols + planes + 2 * cols
    pieces = [piece for piece in ranges(room) if piece[0] == d] or [None]
    many = len(pieces)

    def body(s_ref, *refs):
        block_kernel(
            d, planes, cols, terms, pieces, slots_at, s_ref, refs[0], refs[1 : 1 + many],
            refs[1 + many : 3 + many], refs[-1],
        )

    def held(f, i, s):
        return s[slots_at + planes * 2 * cols + (d * 2 + f) * cols + i]

    def psi_spec(piece):
        if piece is None:
            return pl.BlockSpec(
                (1, 1, width, width),
                lambda f, i, s: (
                    s[2] * 2 + s[3],
                    (s[0] * 2 + (held(f, i, s) // cols ^ s[1])) * cols + held(f, i, s) % cols,
                    0,
                    0,
                ),
            )
        _, first, count = piece

        def index(f, i, s):
            slot = s[slots_at + (d * 2 + f) * cols + i]
            return (jnp.clip(slot - first, 0, count - 1), 0, 0)

        return pl.BlockSpec((1, width, width), index)

    in_specs = [pl.BlockSpec((terms, width, width), lambda f, i, s: (0, 0, 0))]
    in_specs += [psi_spec(piece) for piece in pieces]
    in_specs += [
        pl.BlockSpec(
            (1, 2, per, 1, width, width),
            lambda f, i, s: (held(f, i, s) // cols, 0, 0, held(f, i, s) % cols, 0, 0),
        )
    ] * 2
    inputs = [scalars, left, *psis, *rights]
    aliases = {}
    if beside is not None:
        in_specs.append(pl.BlockSpec(memory_space=pl.ANY))
        aliases = {len(inputs): 0}
        inputs.append(beside)
    blocks = 2 * cols
    return pl.pallas_call(
        body,
        grid_spec=pltpu.PrefetchScalarGridSpec(
            num_scalar_prefetch=1,
            grid=(2, cols),
            in_specs=in_specs,
            out_specs=pl.BlockSpec(
                (1, 1, 1, width, width), lambda f, i, s: (f ^ s[1], (s[0] ^ d) // 2, i, 0, 0)
            ),
        ),
        out_shape=jax.ShapeDtypeStruct((2, 2, cols, width, width), jnp.bfloat16),
        input_output_aliases=aliases,
        compiler_params=pltpu.CompilerParams(vmem_limit_bytes=48 * 2**20),
        cost_estimate=pl.CostEstimate(
            flops=blocks * terms * 16 * width**3,
            bytes_accessed=(terms + blocks * terms + 2 * blocks) * width * width * 2,
            transcendentals=0,
        ),
    )(*inputs)


def put_together(place, own_core, other_core):
    many, cols, width = own_core[0].shape[0], own_core[0].shape[1], own_core[0].shape[-1]

    def body(s_ref, *refs):
        out_ref = refs[-1]
        first = (s_ref[0] + s_ref[3]) % 2 == 0
        for at, mine in ((0, first), (1, jnp.logical_not(first))):

            @pl.when(mine)
            def _(at=at):
                out_ref[0, s_ref[3]] = refs[at][0]
                out_ref[0, 1 - s_ref[3]] = refs[2 + at][0]

    def block_of(at):
        def index(t, s):
            return (jnp.where((s[0] + s[3]) % 2 == at, t, 0), 0, 0, 0)

        return index

    return pl.pallas_call(
        body,
        grid_spec=pltpu.PrefetchScalarGridSpec(
            num_scalar_prefetch=1,
            grid=(many,),
            in_specs=[
                pl.BlockSpec((1, cols, width, width), block_of(at)) for at in (0, 1, 0, 1)
            ],
            out_specs=pl.BlockSpec((1, 2, cols, width, width), lambda t, s: (t, 0, 0, 0, 0)),
        ),
        out_shape=jax.ShapeDtypeStruct((many, 2, cols, width, width), own_core[0].dtype),
    )(place, *own_core, *other_core).reshape(2 * many, cols, width, width)


PIECES = {1: 1, 2: 2, 3: 2}


CUT_STEPS = 2


def ranges(room):
    out = []
    for d, many in PIECES.items():
        ends = [-(-room * at // many) for at in range(many + 1)]
        if many > 1:
            ends[1] += 1
        out += [(d, first, end - first) for first, end in zip(ends[:-1], ends[1:])]
    return out


def cut_out(cells, place, wavefunction, left_ops, planes, room):
    width = wavefunction.shape[-1]
    per = left_ops.shape[0]
    pieces = ranges(room)
    many = len(pieces)
    taken = []
    for to, (d, first, count) in enumerate(pieces):
        each = -(-count // CUT_STEPS)
        taken += [(to, d * room + first, count, each, a) for a in range(each)]

    def body(c_ref, s_ref, *refs):
        half = len(taken) + planes
        t = pl.program_id(0)
        for at, (to, _, count, each, a) in enumerate(taken):
            refs[half + to][jnp.minimum(t * each + a, count - 1)] = refs[at][0, 0]

        @pl.when(t == 0)
        def _():
            kept, to_core, to_chip = refs[half + many :]
            lefts = refs[len(taken) : half]
            kept[...] = lefts[0][:, 0]
            to_core[:per] = lefts[1][:, 0]
            to_core[per:] = lefts[3][:, 0]
            to_chip[...] = lefts[2][:, 0]

    def block_of(to, begin, count, each, a):
        def index(t, c, s):
            return (s[2] * 2 + s[3], c[begin + jnp.minimum(t * each + a, count - 1)], 0, 0)

        return index

    def sector_of(e):
        return lambda t, c, s: (0, (s[2] * 2 + s[3]) ^ e, 0, 0)

    outs = pl.pallas_call(
        body,
        grid_spec=pltpu.PrefetchScalarGridSpec(
            num_scalar_prefetch=2,
            grid=(CUT_STEPS,),
            in_specs=[pl.BlockSpec((1, 1, width, width), block_of(*one)) for one in taken]
            + [pl.BlockSpec((per, 1, width, width), sector_of(e)) for e in range(planes)],
            out_specs=[
                pl.BlockSpec((count, width, width), lambda t, c, s: (0, 0, 0))
                for _, _, count in pieces
            ]
            + [
                pl.BlockSpec((per * many, width, width), lambda t, c, s: (0, 0, 0))
                for many in (1, 2, 1)
            ],
        ),
        out_shape=[
            jax.ShapeDtypeStruct((count, width, width), wavefunction.dtype)
            for _, _, count in pieces
        ]
        + [
            jax.ShapeDtypeStruct((per * many, width, width), left_ops.dtype) for many in (1, 2, 1)
        ],
        compiler_params=pltpu.CompilerParams(vmem_limit_bytes=48 * 2**20),
    )(cells, place, *([wavefunction] * len(taken)), *([left_ops] * planes))
    return outs[:many], outs[many:]


def running(mask):
    size = mask.shape[-1]
    upto = jnp.arange(size)[:, None] >= jnp.arange(size)[None, :]
    return jnp.sum(jnp.where(upto, mask[..., None, :], 0), axis=-1)


def planned(
    room, place, cell_table, left_sizes, right_sizes, links, wavefunction, left_ops, right_ops
):
    planes = lax.axis_size("z")
    z = lax.axis_index("z")
    sectors = wavefunction.shape[1]
    width = wavefunction.shape[-1]
    cols = sectors // planes // 2
    after = lax.optimization_barrier

    def inner(value):
        return lax.ppermute(value, "z", [(1, 2), (2, 1)])

    def outer(value):
        return lax.ppermute(value, "z", [(1, 0), (2, 3)])

    def flip(value, axis, bit):
        size = lax.axis_size(axis)
        return lax.ppermute(value, axis, [(i, i ^ bit) for i in range(size)])

    per = left_ops.shape[0]
    scalars = kernel_scalars(place, wavefunction.shape[0], left_sizes, right_sizes, links)
    cells = cell_table[:, :room].reshape(-1)
    cuts, sectors_cut = cut_out(cells, place, wavefunction, left_ops, planes, room)
    cuts, sectors_cut, right_ops = after((cuts, sectors_cut, right_ops))
    kept, to_core, to_chip = sectors_cut
    from_core = flip(to_core, "c", 1)
    from_chip = flip(jnp.concatenate([to_chip, from_core[per:]], axis=0), "x", 1)
    mine = [kept, from_core[:per], from_chip]
    psis = {0: [wavefunction]}
    late = cuts[-1]
    for (d, _, _), cut in zip(ranges(room)[:-1], cuts):
        psis.setdefault(d, []).append(flip(cut, "z", d))
    r_y = flip(right_ops, "y", 1)
    r_x1 = flip(right_ops[: per // 2], "x", 1)
    rest = right_ops[per // 2 :]
    mine, rest, r_y, r_x1, psis[1], psis[2][0] = after((mine, rest, r_y, r_x1, psis[1], psis[2][0]))
    r_x2 = flip(rest, "x", 1)
    r_xy = flip(r_y, "x", 1)
    own = jnp.concatenate(mine, axis=0)
    beside = flip(own, "z", 1)
    inner1 = inner(own)
    beside, inner1, r_x2, r_xy, psis[2][1] = after((beside, inner1, r_x2, r_xy, psis[2][1]))
    r_x = jnp.concatenate([r_x1, r_x2], axis=0)
    near = jnp.stack([right_ops, r_x, r_y, r_xy]).reshape(2, 2, *right_ops.shape)
    other = flip(near, "c", 1)
    inner2 = inner(beside)
    outer1 = outer(inner1)
    rights = [near, other]
    lefts = [own, beside, None, None]
    firsts = [
        multiply(first, room, scalars, lefts[first], psis[first], rights) for first, _ in GROUPS
    ]
    inner2, outer1, firsts, late, psis[3][0] = after((inner2, outer1, firsts, late, psis[3][0]))
    outer2 = outer(inner2)
    psis[3].append(flip(late, "z", 3))

    inside = (z == 1) | (z == 2)
    lefts[2] = jnp.where(inside, inner2, outer1)
    lefts[3] = jnp.where(inside, inner1, outer2)

    own_core, other_core = [], []
    for (_, second), done in zip(GROUPS, firsts):
        done = multiply(second, room, scalars, lefts[second], psis[second], rights, done)
        done = done.reshape(4, cols, width, width)
        own_core.append(
            lax.all_to_all(done, ("y", "x"), split_axis=0, concat_axis=0, tiled=True)
        )
        other_core.append(flip(own_core[-1], "c", 1))
    return put_together(place, own_core, other_core)


def tables(wavefunction, links):
    planes = lax.axis_size("z")
    z, y, x, c = (lax.axis_index(name) for name in ("z", "y", "x", "c"))
    owned, sectors = wavefunction.shape[:2]
    plane_cols = sectors // planes
    o = x * 2 + c
    place = jnp.stack([z, y, x, c]).astype(jnp.int32)
    flips = jnp.arange(planes)
    marks = (links != 0).astype(jnp.int32)
    by_row = marks.reshape(planes, 2, owned, planes, plane_cols)
    away = (flips[:, None] != flips[None, :])[:, None, None, :]
    most = jnp.max(jnp.where(away, jnp.sum(by_row, axis=-1), 0))

    sent = marks[(z * 2 + y) * owned + o].reshape(planes, plane_cols)[z ^ flips]
    slot = running(sent) - 1
    hit = (slot[:, None, :] == jnp.arange(plane_cols)[None, :, None]) & (sent[:, None, :] > 0)
    sector = (z ^ flips)[:, None] * plane_cols + jnp.arange(plane_cols)[None, :]
    cell_table = jnp.sum(jnp.where(hit, sector[:, None, :], 0), axis=-1).astype(jnp.int32)

    return most, place, cell_table


def kernel_scalars(place, owned, left_sizes, right_sizes, links):
    planes = lax.axis_size("z")
    z, y, x, c = (lax.axis_index(name) for name in ("z", "y", "x", "c"))
    plane_cols = links.shape[1] // planes
    cols = plane_cols // 2
    marks = (links != 0).astype(jnp.int32)

    q_of = ((z ^ jnp.arange(planes)) * 2 + y) * owned + x * 2 + c
    come = lax.dynamic_slice_in_dim(marks[q_of], z * plane_cols, plane_cols, 1)
    slots = jnp.maximum(running(come) - 1, 0)

    def sided(table):
        table = table.reshape(planes, 2, cols)
        return jnp.where(y > 0, table[:, ::-1], table).reshape(planes, plane_cols)

    flags = sided(come)
    steps = jnp.arange(plane_cols)
    upto = (steps[:, None] >= steps[None, :]) & (flags[:, None, :] > 0)
    last = jnp.max(jnp.where(upto, steps, -1), axis=-1)
    first = jnp.min(jnp.where(flags > 0, steps, plane_cols - 1), axis=-1)
    held = jnp.where(last >= 0, last, first[:, None])
    r_of = (z * 2 + (y ^ jnp.arange(2)))[:, None] * cols + jnp.arange(cols)[None, :]
    parts = [place, flags, left_sizes[q_of], right_sizes[r_of.reshape(-1)], sided(slots), held]
    return jnp.concatenate([part.reshape(-1) for part in parts]).astype(jnp.int32)


ROOMS = (5, 6, 7)


def sparse(wavefunction, left_ops, right_ops, left_sizes, right_sizes, links):
    most, *rest = tables(wavefunction, links)
    rest += [left_sizes, right_sizes, links]
    whole = wavefunction.shape[1] // lax.axis_size("z")
    rooms = [room for room in ROOMS if room < whole] + [whole]
    forms = [functools.partial(planned, room) for room in rooms]
    which = jnp.sum((most > jnp.array(rooms[:-1], jnp.int32)).astype(jnp.int32))
    return lax.switch(which, forms, *rest, wavefunction, left_ops, right_ops)


def solution(mesh):
    sec, ops = mesh.shape["sec"], mesh.shape["ops"]

    def run(wavefunction, *rest):
        sectors = wavefunction.shape[0]
        if ops == 4 and sec == 2 * ops and sectors == sec * ops:
            where = Mesh(mesh.devices.reshape(sec // 2, 2, ops // 2, 2), ("z", "y", "x", "c"))
            side, group, body = ("z", "y"), ("x", "c"), sparse
        else:
            where, side, group, body = mesh, "sec", "ops", generic
        placed = (
            P(side, None, None, None),
            P(group, side, None, None),
            P(group, side, None, None),
            P(),
            P(),
            P(),
        )
        return jax.shard_map(
            body, mesh=where, in_specs=placed, out_specs=P(group, side, None, None), check_vma=False
        )(wavefunction, *rest)

    return run
```
